32 devices in a mesh: seq: 32 (over z, y, x, core).
Axes of the slice: x: 2, y: 2, z: 4, core: 2. Of those that a mesh axis runs over, the one named last changes fastest.
Arguments:
- tokens: bfloat16 [16384, 1536], P('seq'), may hold values from -6 to 6
- norm_gain: float32 [1536], replicated, may hold values from 0.5 to 1.5
- w_query: bfloat16 [1536, 1536], replicated
- w_key_value: bfloat16 [1536, 256], replicated
- w_out: bfloat16 [1536, 1536], replicated, may hold values from -1.75 to 1.75
- segment_ids: int32 [16384], P('seq'), may hold values from 0 to 15, as said below
- page_owner: int32 [1024], P('seq'), may hold values from 0 to 31, as said below
- page_slot: int32 [1024], P('seq'), may hold values from 0 to 31, as said below
Outputs:
- attn_out: bfloat16 [16384, 1536], P('seq')
- kv_cache: bfloat16 [16384, 256], P('seq')
The draws below stay inside these ranges and needn't reach their ends.
Inputs may be any that keep to these rules, and one draw needn't show every extreme that they name: `segment_ids`: segments are contiguous runs of the stream, never falling, each of 1 to 4096 tokens; one has exactly 4096. `page_owner`: the 32 pages of one device go to different owners; some owner keeps a page of every device. `page_slot`: two pages with the same owner have different slots.
All inputs are finite; a program needn't handle non-finite values.
Results may differ from the reference program's by a relative error of at most 0.0086.
Values may be sent and summed in bfloat16 or wider, within the bound.
A program may use at most 256 MiB of HBM per device.

```python
import jax
import jax.numpy as jnp
from jax import lax

D = 1536
HEADS = 12
HEAD_DIM = 128
WINDOW = 1024
MAXLEN = 4096
PAGE = 16
TOK_DEV = 512
TOKENS = 16384
DOCS = 16
PAGES = 1024
REACH = 2
CACHE_ROWS = 16384
N_SEQ = 32


def shared_key_rows(key):
    return jax.random.normal(jax.random.fold_in(key, 11), (D, HEAD_DIM), jnp.float32) * D ** (-0.5)


def draw_w_query(key, part):
    weights_all = jax.random.normal(jax.random.fold_in(key, 14), (D, HEADS, HEAD_DIM), jnp.float32) * D ** (-0.5)
    return weights_all.reshape(D, HEADS * HEAD_DIM).astype(jnp.bfloat16)


def draw_w_key_value(key, part):
    key_rows = shared_key_rows(key)
    value_rows = jax.random.normal(jax.random.fold_in(key, 16), (D, HEAD_DIM), jnp.float32) * D ** (-0.5)
    return jnp.concatenate([key_rows, value_rows], 1).astype(jnp.bfloat16)


def draw_segment_ids(key, part):
    band = MAXLEN // 4
    cut_index = jnp.arange(1, DOCS, dtype=jnp.int32)
    jitter = jax.random.randint(jax.random.fold_in(key, 41), (DOCS - 1,), 0, band)
    cuts = cut_index * band - band // 2 + jitter
    middle = N_SEQ // 2 * TOK_DEV
    middle_band = middle // band
    reach_back = min(TOK_DEV, band // 2)
    first_offset = jax.random.randint(jax.random.fold_in(key, 42), (), 1, reach_back)
    second_offset = jax.random.randint(jax.random.fold_in(key, 43), (), 1, reach_back)
    cuts = jnp.where(cut_index == middle_band, middle - reach_back + first_offset, cuts)
    cuts = jnp.where(cut_index == middle_band + 1, middle + second_offset, cuts)
    tail_start = TOKENS - 4 * band
    gaps = jax.random.randint(jax.random.fold_in(key, 44), (3,), 1, band // 8 + 1)
    cuts = jnp.where(cut_index == DOCS - 1, tail_start, cuts)
    cuts = jnp.where(cut_index == DOCS - 2, tail_start - gaps[0], cuts)
    cuts = jnp.where(cut_index == DOCS - 3, tail_start - gaps[0] - gaps[1], cuts)
    cuts = jnp.where(cut_index == DOCS - 4, tail_start - gaps[0] - gaps[1] - gaps[2], cuts)
    stream_index = jnp.arange(TOKENS, dtype=jnp.int32)
    segment_numbers = jnp.sum((stream_index[:, None] >= cuts[None, :]).astype(jnp.int32), 1)
    return segment_numbers.astype(jnp.int32)


def page_table(key):
    devices = N_SEQ
    per_device = TOK_DEV // PAGE
    busy_owner = jax.random.randint(jax.random.fold_in(key, 31), (), 0, devices)
    owner_keys = jax.random.split(jax.random.fold_in(key, 32), devices)
    others = jax.vmap(lambda subkey: jax.random.permutation(subkey, devices - 1))(owner_keys)[:, :per_device - 1] + 1
    chosen = jnp.concatenate([jnp.zeros((devices, 1), jnp.int32), others.astype(jnp.int32)], 1)
    order_keys = jax.random.split(jax.random.fold_in(key, 33), devices)
    page_order = jax.vmap(lambda subkey: jax.random.permutation(subkey, per_device))(order_keys)
    chosen = jnp.take_along_axis(chosen, page_order, 1)
    owners = (busy_owner + chosen) % devices
    slot_keys = jax.random.split(jax.random.fold_in(key, 34), devices)
    slot_perm = jax.vmap(lambda subkey: jax.random.permutation(subkey, devices))(slot_keys)
    sources = jnp.broadcast_to(jnp.arange(devices, dtype=jnp.int32)[:, None], owners.shape)
    slot_ids = slot_perm[owners, sources]
    return (owners.reshape(-1).astype(jnp.int32), slot_ids.reshape(-1).astype(jnp.int32))


def draw_page_owner(key, part):
    return page_table(key)[0]


def draw_page_slot(key, part):
    return page_table(key)[1]


def level_of(stream_key, dims, cuts, low, largest):
    loudness = 1.0
    for position, shards_of in cuts:
        draws = jax.random.uniform(jax.random.fold_in(jax.random.fold_in(stream_key, 6), position), (shards_of,), jnp.float32, low / len(cuts), largest / len(cuts))
        loudness = loudness * jnp.repeat(jnp.exp(draws), dims[position] // shards_of).reshape((-1,) + (1,) * (len(dims) - 1 - position))
    return loudness


def noise(rng, extent, spread, reach, cuts=(), kind=jnp.bfloat16):
    loudness = level_of(rng, extent, cuts, -0.22, 0.18) if cuts else 1.0
    result = jax.random.normal(rng, extent, jnp.float32) * spread * loudness
    return jnp.minimum(jnp.maximum(result, -reach), reach).astype(kind)


def setup_inputs(seed: int = 0) -> dict:
    key_of = jax.random.split(jax.random.key(seed), 9)
    tokens = noise(key_of[0], (TOKENS, D), 1.0, 6.0, ((0, 32),))
    norm_gain = jnp.clip(1.0 + 0.1 * jax.random.normal(key_of[1], (D,), jnp.float32), 0.5, 1.5)
    w_query = draw_w_query(jax.random.fold_in(key_of[8], 71), 0)
    w_key_value = draw_w_key_value(jax.random.fold_in(key_of[8], 71), 0)
    w_out = noise(key_of[4], (HEADS * HEAD_DIM, D), HEADS ** -0.5, 1.75)
    segment_ids = draw_segment_ids(jax.random.fold_in(key_of[8], 71), 0)
    page_owner = draw_page_owner(jax.random.fold_in(key_of[8], 71), 0)
    page_slot = draw_page_slot(jax.random.fold_in(key_of[8], 71), 0)
    return dict(tokens=tokens, norm_gain=norm_gain, w_query=w_query, w_key_value=w_key_value, w_out=w_out, segment_ids=segment_ids, page_owner=page_owner, page_slot=page_slot)


EPS = 1e-06
ROPE_BASE = 10000.0

def rotate(vectors, positions):
    width = vectors.shape[-1]
    half_dim = width // 2
    pair_index = jnp.arange(half_dim, dtype=jnp.float32)
    frequency = ROPE_BASE ** (-2.0 * pair_index / width)
    angles = positions.astype(jnp.float32)[:, None] * frequency[None, :]
    if vectors.ndim == 3:
        angles = angles[:, None, :]
    cosine = jnp.cos(angles)
    sine_part = jnp.sin(angles)
    first_half = vectors[..., :half_dim]
    second_half = vectors[..., half_dim:]
    return jnp.concatenate([first_half * cosine - second_half * sine_part, second_half * cosine + first_half * sine_part], -1)

def reference(tokens, norm_gain, w_query, w_key_value, w_out, segment_ids, page_owner, page_slot):
    stream_index = jnp.arange(TOKENS, dtype=jnp.int32)
    change = jnp.concatenate([jnp.ones((1,), dtype=jnp.bool_), segment_ids[1:] != segment_ids[:-1]])
    starts = lax.cummax(jnp.where(change, stream_index, 0).astype(jnp.int32))
    positions = stream_index - starts
    wide = tokens.astype(jnp.float32)
    mean_square = lax.optimization_barrier(jnp.mean(wide * wide, -1, keepdims=True))
    normed = (wide * lax.rsqrt(mean_square + EPS) * norm_gain).astype(jnp.bfloat16)
    queries = jnp.dot(normed, w_query, preferred_element_type=jnp.float32).reshape(TOKENS, HEADS, HEAD_DIM)
    queries = (rotate(queries, positions) * HEAD_DIM ** (-0.5)).astype(jnp.bfloat16)
    projected = jnp.dot(normed, w_key_value, preferred_element_type=jnp.float32)
    keyval = jnp.concatenate([rotate(projected[:, :HEAD_DIM], positions), projected[:, HEAD_DIM:]], 1).astype(jnp.bfloat16)
    padded = jnp.concatenate([jnp.zeros((REACH * TOK_DEV, 2 * HEAD_DIM), jnp.bfloat16), keyval], 0)
    span = (REACH + 1) * TOK_DEV

    def attend(block_index):
        begin = (block_index * TOK_DEV).astype(jnp.int32)
        block_queries = lax.dynamic_slice_in_dim(queries, begin, TOK_DEV, 0).astype(jnp.float32)
        block_starts = lax.dynamic_slice_in_dim(starts, begin, TOK_DEV, 0)
        key_rows = lax.dynamic_slice_in_dim(padded, begin, span, 0).astype(jnp.float32)
        query_index = begin + jnp.arange(TOK_DEV, dtype=jnp.int32)
        key_index = begin - REACH * TOK_DEV + jnp.arange(span, dtype=jnp.int32)
        valid = (key_index[None, :] >= block_starts[:, None]) & (key_index[None, :] <= query_index[:, None]) & (query_index[:, None] - key_index[None, :] < WINDOW)
        scores = jnp.einsum('thd,kd->thk', block_queries, key_rows[:, :HEAD_DIM])
        scores = jnp.where(valid[:, None, :], scores, -1e+30)
        row_peak = lax.optimization_barrier(jnp.max(scores, 2, keepdims=True))
        exponent = jnp.exp(scores - row_peak)
        probs = (exponent / lax.optimization_barrier(jnp.sum(exponent, 2, keepdims=True))).astype(jnp.bfloat16)
        context = jnp.einsum('thk,kd->thd', probs.astype(jnp.float32), key_rows[:, HEAD_DIM:])
        return context.astype(jnp.bfloat16).reshape(TOK_DEV, HEADS * HEAD_DIM)
    context = lax.map(attend, jnp.arange(N_SEQ, dtype=jnp.int32)).reshape(TOKENS, HEADS * HEAD_DIM)
    attn_out = jnp.dot(context, w_out, preferred_element_type=jnp.float32).astype(jnp.bfloat16)
    page_rows = keyval.reshape(PAGES, PAGE, 2 * HEAD_DIM)
    targets = (page_owner * N_SEQ + page_slot).astype(jnp.int32)
    cache = jnp.zeros((N_SEQ * N_SEQ, PAGE, 2 * HEAD_DIM), jnp.bfloat16).at[targets].set(page_rows)
    return (attn_out, cache.reshape(CACHE_ROWS, 2 * HEAD_DIM))
```

```python
import functools
import math

import jax
import jax.numpy as jnp
import numpy as np
from jax import lax
from jax.experimental import pallas as pl
from jax.experimental.pallas import tpu as pltpu
from jax.sharding import PartitionSpec as P

WINDOW = 1024
MAXLEN = 4096
PAGE = 16
EPS = 1e-06
ROPE_BASE = 10000.0
LANES = 128
QUERY_TILE = 128
HEAD_GROUP = 4
MESH = pl.DeviceIdType.MESH


def cos_sin(angles):
    turns = jnp.floor(angles * (2.0 / math.pi) + 0.5)
    c1 = 1.5703125
    c2 = float(np.float32(4.837512969970703125e-4))
    c3 = float(np.float32(7.54978995489188216e-8))
    r = ((angles - turns * c1) - turns * c2) - turns * c3
    r2 = r * r
    s = r * (1.0 + r2 * (-1.0 / 6 + r2 * (1.0 / 120 + r2 * (-1.0 / 5040))))
    c = 1.0 + r2 * (-0.5 + r2 * (1.0 / 24 + r2 * (-1.0 / 720 + r2 * (1.0 / 40320))))
    quadrant = turns.astype(jnp.int32) & 3
    odd = (quadrant & 1) == 1
    cosine = jnp.where(odd, s, c)
    sine = jnp.where(odd, c, s)
    cosine = jnp.where((quadrant == 1) | (quadrant == 2), -cosine, cosine)
    sine = jnp.where(quadrant >= 2, -sine, sine)
    return cosine, sine


def column_of(row):
    shape = (LANES, LANES)
    diagonal = lax.broadcasted_iota(jnp.int32, shape, 0) == lax.broadcasted_iota(jnp.int32, shape, 1)
    return jnp.sum(jnp.where(diagonal, jnp.broadcast_to(row, shape), 0), 1, keepdims=True)


def spread(column, count):
    shape = (count, count * PAGE)
    lane = lax.broadcasted_iota(jnp.int32, shape, 1)
    mine = (lane // PAGE) == lax.broadcasted_iota(jnp.int32, shape, 0)
    row = jnp.sum(jnp.where(mine, column, 0), 0, keepdims=True)
    return row * PAGE + lax.broadcasted_iota(jnp.int32, (1, count * PAGE), 1) % PAGE


def one_hot_rows(targets, first, rows):
    row = first + lax.broadcasted_iota(jnp.int32, (rows, targets.shape[1]), 0)
    return jnp.where(row == targets, 1.0, 0.0).astype(jnp.bfloat16)


def exchange_kernel(
    devices, pages, reach, back,
    table_ref, frequency_ref, gain_ref, tokens_ref, w_kv_ref, w_query_ref,
    query_out, kv_out, low_out, cache_out,
    tokens_buf, w_kv_buf, w_query_buf, normed, kv_own, kv_in, tables, send_pages, got_pages,
    cosine, sine, load_sem, table_send, table_recv, page_send, page_recv, kv_send, kv_recv,
):
    me = lax.axis_index("seq")
    rows = tokens_buf.shape[0]
    head_dim = kv_own.shape[1] // 2
    seg_rows = rows // LANES
    loads = [
        pltpu.make_async_copy(tokens_ref, tokens_buf, load_sem.at[0]),
        pltpu.make_async_copy(w_kv_ref, w_kv_buf, load_sem.at[1]),
        pltpu.make_async_copy(w_query_ref, w_query_buf, load_sem.at[2]),
    ]
    for load in loads:
        load.start()

    barrier = pltpu.get_barrier_semaphore()

    def greet(k, carry):
        pl.semaphore_signal(
            barrier, inc=1, device_id=(lax.rem(me + k, devices),), device_id_type=MESH
        )
        return carry

    lax.fori_loop(1, devices, greet, 0)
    pl.semaphore_wait(barrier, devices - 1)

    def send_table(k, carry):
        pltpu.make_async_remote_copy(
            src_ref=table_ref, dst_ref=tables.at[k - 1], send_sem=table_send, recv_sem=table_recv,
            device_id=(lax.rem(me + k, devices),), device_id_type=MESH,
        ).start()
        return carry

    lax.fori_loop(1, devices, send_table, 0)
    tables[devices - 1] = table_ref[...]

    loads[0].wait()
    step = 128

    def norm_tile(i, carry):
        at = pl.ds(pl.multiple_of(i * step, step), step)
        wide = tokens_buf[at, :].astype(jnp.float32)
        mean_square = jnp.mean(wide * wide, -1, keepdims=True)
        normed[at, :] = (wide * lax.rsqrt(mean_square + EPS) * gain_ref[...]).astype(jnp.bfloat16)
        return carry

    lax.fori_loop(0, rows // step, norm_tile, 0)
    loads[1].wait()
    projected = jnp.dot(normed[...], w_kv_buf[...], preferred_element_type=jnp.float32)

    table = table_ref[...]
    ids = jnp.concatenate([column_of(table[r : r + 1, :]) for r in range(seg_rows)], 0)
    below = jnp.zeros((rows, LANES), jnp.int32)
    for r in range(seg_rows):
        below = below + jnp.where(table[r : r + 1, :] < ids, 1, 0)
    local_start = jnp.sum(below, 1, keepdims=True)
    owner_column = column_of(table[seg_rows : seg_rows + 1, :])[:pages]
    order = one_hot_rows(spread(owner_column, pages), 0, devices * PAGE)

    blocks = tables.at[pl.ds(0, devices - 1)]
    pltpu.make_async_copy(blocks, blocks, table_recv).wait()
    first_id = table[0:1, 0:1]
    earlier = jnp.zeros((seg_rows, LANES), jnp.int32)
    for k in range(1, min(back, devices - 1) + 1):
        present = jnp.where(me >= k, 1, 0)
        earlier = earlier + jnp.where(tables[k - 1, 0:seg_rows, :] == first_id, present, 0)
    before = jnp.sum(jnp.sum(earlier, 1, keepdims=True), 0, keepdims=True)
    local_index = lax.broadcasted_iota(jnp.int32, (rows, 1), 0)
    start = local_start - jnp.where(ids == first_id, before, 0)
    positions = local_index - start
    low = jnp.maximum(start, local_index - (WINDOW - 1)) + reach * rows
    low_out[...] = jnp.broadcast_to(low, low_out.shape)

    angles = positions.astype(jnp.float32) * frequency_ref[...]
    cos_part, sin_part = cos_sin(angles)
    lane = lax.broadcasted_iota(jnp.int32, (rows, head_dim), 1)
    cosine[...] = cos_part
    sine[...] = jnp.where(lane < head_dim // 2, -sin_part, sin_part)

    def rotate(v):
        return v * cosine[...] + pltpu.roll(v, head_dim // 2, 1) * sine[...]

    kv_own[:, :head_dim] = rotate(projected[:, :head_dim]).astype(jnp.bfloat16)
    kv_own[:, head_dim:] = projected[:, head_dim:].astype(jnp.bfloat16)
    kv_copies = []
    for hop in range(1, reach + 1):
        copy = pltpu.make_async_remote_copy(
            src_ref=kv_own, dst_ref=kv_in.at[reach - hop],
            send_sem=kv_send.at[hop - 1], recv_sem=kv_recv.at[hop - 1],
            device_id=(lax.rem(me + hop, devices),), device_id_type=MESH,
        )
        copy.start()
        kv_copies.append(copy)
    send_pages[...] = (
        jnp.dot(order, kv_own[...], preferred_element_type=jnp.float32)
        .astype(jnp.bfloat16)
        .reshape(send_pages.shape)
    )

    def send_page(k, carry):
        to = lax.rem(me + k, devices)
        pltpu.make_async_remote_copy(
            src_ref=send_pages.at[to], dst_ref=got_pages.at[k - 1],
            send_sem=page_send, recv_sem=page_recv,
            device_id=(to,), device_id_type=MESH,
        ).start()
        return carry

    lax.fori_loop(1, devices, send_page, 0)
    got_pages[devices - 1] = send_pages[me]

    loads[2].wait()
    pair = 2 * head_dim
    scale = head_dim ** (-0.5) * math.log2(math.e)

    def query_pair(j, carry):
        columns = pl.ds(pl.multiple_of(j * pair, pair), pair)
        part = jnp.dot(normed[...], w_query_buf[:, columns], preferred_element_type=jnp.float32)
        query_out[2 * j] = (rotate(part[:, :head_dim]) * scale).astype(jnp.bfloat16)
        query_out[2 * j + 1] = (rotate(part[:, head_dim:]) * scale).astype(jnp.bfloat16)
        return carry

    lax.fori_loop(0, query_out.shape[0] // 2, query_pair, 0)

    kv_out[reach * rows :, :] = kv_own[...]
    owners = tables[:, seg_rows, :]
    slots = tables[:, seg_rows + 1, :]
    slot_column = jnp.sum(jnp.where(owners == me, slots + 1, 0), 1, keepdims=True) - 1
    targets = spread(slot_column, devices)

    pages_in = got_pages.at[pl.ds(0, devices - 1)]
    pltpu.make_async_copy(pages_in, pages_in, page_recv).wait()
    got = got_pages[...].reshape(devices * PAGE, 2 * head_dim)
    chunk = min(512, cache_out.shape[0])
    for c in range(cache_out.shape[0] // chunk):
        place = one_hot_rows(targets, c * chunk, chunk)
        cache_out[c * chunk : (c + 1) * chunk, :] = jnp.dot(
            place, got, preferred_element_type=jnp.float32
        ).astype(jnp.bfloat16)
    for hop in range(1, reach + 1):
        kv_copies[hop - 1].wait()
    for slot in range(reach):
        kv_out[slot * rows : (slot + 1) * rows, :] = kv_in[slot]
    pltpu.make_async_copy(blocks, blocks, table_send).wait()
    pltpu.make_async_copy(pages_in, pages_in, page_send).wait()


def attention_kernel(query_ref, kv_ref, low_ref, w_out_ref, out_ref, context, value_sum, bias, w_buf, sem):
    heads, rows, head_dim = query_ref.shape
    load = pltpu.make_async_copy(w_out_ref, w_buf, sem)
    load.start()
    span = WINDOW + QUERY_TILE
    value_sum[:, :head_dim] = kv_ref[:, head_dim:]
    value_sum[:, head_dim:] = jnp.ones((kv_ref.shape[0], head_dim), jnp.bfloat16)
    extra = kv_ref.shape[0] - rows

    def tile(i, carry):
        first = pl.multiple_of(i * QUERY_TILE, QUERY_TILE)
        at = pl.ds(first, QUERY_TILE)
        shape = (QUERY_TILE, span)
        key_row = first + (extra - WINDOW) + lax.broadcasted_iota(jnp.int32, shape, 1)
        query_row = first + extra + lax.broadcasted_iota(jnp.int32, shape, 0)
        low = low_ref[at, 0:1]
        bias[...] = jnp.where((key_row >= low) & (key_row <= query_row), 0.0, -1e30)
        key_at = pl.ds(pl.multiple_of(first + (extra - WINDOW), QUERY_TILE), span)

        def group(g, carry):
            for j in range(HEAD_GROUP):
                h = g * HEAD_GROUP + j
                scores = lax.dot_general(
                    query_ref[h, at, :], kv_ref[key_at, :head_dim],
                    (((1,), (1,)), ((), ())), preferred_element_type=jnp.float32,
                ) + bias[...]
                peak = jnp.max(scores, 1, keepdims=True)
                weights = jnp.exp2(scores - peak).astype(jnp.bfloat16)
                both = jnp.dot(weights, value_sum[key_at, :], preferred_element_type=jnp.float32)
                context[h, at, :] = (both[:, :head_dim] / both[:, head_dim:]).astype(jnp.bfloat16)
            return carry

        lax.fori_loop(0, heads // HEAD_GROUP, group, 0)
        return carry

    lax.fori_loop(0, rows // QUERY_TILE, tile, 0)
    load.wait()
    whole = jnp.concatenate([context[h] for h in range(heads)], 1)
    width = 256

    def column(j, carry):
        columns = pl.ds(pl.multiple_of(j * width, width), width)
        out_ref[:, columns] = jnp.dot(
            whole, w_buf[:, columns], preferred_element_type=jnp.float32
        ).astype(jnp.bfloat16)
        return carry

    lax.fori_loop(0, out_ref.shape[1] // width, column, 0)


def body(devices, tokens, norm_gain, w_query, w_key_value, w_out, segment_ids, page_owner, page_slot):
    rows, width = tokens.shape
    head_dim = w_key_value.shape[1] // 2
    heads = w_query.shape[1] // head_dim
    pages = rows // PAGE
    reach = WINDOW // rows
    back = MAXLEN // rows
    bf16, f32 = jnp.bfloat16, jnp.float32
    pad = jnp.full((LANES - pages,), -1, jnp.int32)
    seg_rows = rows // LANES
    table = jnp.concatenate(
        [segment_ids, page_owner, pad, page_slot, pad, jnp.zeros(((6 - seg_rows) * LANES,), jnp.int32)]
    ).reshape(8, LANES)
    half = ROPE_BASE ** (-2.0 * np.arange(head_dim // 2, dtype=np.float64) / head_dim)
    frequency = jnp.asarray(np.concatenate([half, half])[None, :].astype(np.float32))
    vmem = pl.BlockSpec(memory_space=pltpu.VMEM)
    anywhere = pl.BlockSpec(memory_space=pl.ANY)
    dma = pltpu.SemaphoreType.DMA
    query, kv_all, low, cache = pl.pallas_call(
        functools.partial(exchange_kernel, devices, pages, reach, back),
        out_shape=(
            jax.ShapeDtypeStruct((heads, rows, head_dim), bf16),
            jax.ShapeDtypeStruct(((reach + 1) * rows, 2 * head_dim), bf16),
            jax.ShapeDtypeStruct((rows, LANES), jnp.int32),
            jax.ShapeDtypeStruct((devices * PAGE, 2 * head_dim), bf16),
        ),
        in_specs=[vmem, vmem, vmem, anywhere, anywhere, anywhere],
        out_specs=(vmem, vmem, vmem, vmem),
        scratch_shapes=[
            pltpu.VMEM((rows, width), bf16),
            pltpu.VMEM(w_key_value.shape, bf16),
            pltpu.VMEM(w_query.shape, bf16),
            pltpu.VMEM((rows, width), bf16),
            pltpu.VMEM((rows, 2 * head_dim), bf16),
            pltpu.VMEM((reach, rows, 2 * head_dim), bf16),
            pltpu.VMEM((devices, 8, LANES), jnp.int32),
            pltpu.VMEM((devices, PAGE, 2 * head_dim), bf16),
            pltpu.VMEM((devices, PAGE, 2 * head_dim), bf16),
            pltpu.VMEM((rows, head_dim), f32),
            pltpu.VMEM((rows, head_dim), f32),
            dma((3,)),
            dma, dma, dma, dma,
            dma((reach,)), dma((reach,)),
        ],
        compiler_params=pltpu.CompilerParams(
            collective_id=0, has_side_effects=True, vmem_limit_bytes=48 * 1024 * 1024
        ),
        name="project_and_exchange",
    )(table, frequency, norm_gain.reshape(1, width), tokens, w_key_value, w_query)
    attn_out = pl.pallas_call(
        attention_kernel,
        out_shape=jax.ShapeDtypeStruct((rows, w_out.shape[1]), bf16),
        in_specs=[vmem, vmem, vmem, anywhere],
        out_specs=vmem,
        scratch_shapes=[
            pltpu.VMEM((heads, rows, head_dim), bf16),
            pltpu.VMEM(((reach + 1) * rows, 2 * head_dim), bf16),
            pltpu.VMEM((QUERY_TILE, WINDOW + QUERY_TILE), f32),
            pltpu.VMEM(w_out.shape, bf16),
            dma,
        ],
        compiler_params=pltpu.CompilerParams(vmem_limit_bytes=48 * 1024 * 1024),
        name="attend_and_project",
    )(query, kv_all, low, w_out)
    return attn_out, cache


def solution(mesh):
    placed = (P("seq", None), P(), P(), P(), P(), P("seq"), P("seq"), P("seq"))
    return jax.shard_map(
        functools.partial(body, mesh.shape["seq"]),
        mesh=mesh,
        in_specs=placed,
        out_specs=(P("seq", None), P("seq", None)),
        check_vma=False,
    )
```

```python
import functools
import math

import jax
import jax.numpy as jnp
import numpy as np
from jax import lax
from jax.experimental import pallas as pl
from jax.experimental.pallas import tpu as pltpu
from jax.sharding import PartitionSpec as P

WINDOW = 1024
MAXLEN = 4096
PAGE = 16
EPS = 1e-06
ROPE_BASE = 10000.0
LANES = 128
QUERY_TILE = 128
HEAD_GROUP = 2
MESH = pl.DeviceIdType.MESH


def cos_sin(angles):
    turns = jnp.floor(angles * (2.0 / math.pi) + 0.5)
    c1 = 1.5703125
    c2 = float(np.float32(4.837512969970703125e-4))
    c3 = float(np.float32(7.54978995489188216e-8))
    r = ((angles - turns * c1) - turns * c2) - turns * c3
    r2 = r * r
    s = r * (1.0 + r2 * (-1.0 / 6 + r2 * (1.0 / 120 + r2 * (-1.0 / 5040))))
    c = 1.0 + r2 * (-0.5 + r2 * (1.0 / 24 + r2 * (-1.0 / 720 + r2 * (1.0 / 40320))))
    quadrant = turns.astype(jnp.int32) & 3
    odd = (quadrant & 1) == 1
    cosine = jnp.where(odd, s, c)
    sine = jnp.where(odd, c, s)
    cosine = jnp.where((quadrant == 1) | (quadrant == 2), -cosine, cosine)
    sine = jnp.where(quadrant >= 2, -sine, sine)
    return cosine, sine


def column_of(row):
    shape = (LANES, LANES)
    diagonal = lax.broadcasted_iota(jnp.int32, shape, 0) == lax.broadcasted_iota(jnp.int32, shape, 1)
    return jnp.sum(jnp.where(diagonal, jnp.broadcast_to(row, shape), 0), 1, keepdims=True)


def spread(column, count):
    shape = (count, count * PAGE)
    lane = lax.broadcasted_iota(jnp.int32, shape, 1)
    mine = (lane // PAGE) == lax.broadcasted_iota(jnp.int32, shape, 0)
    row = jnp.sum(jnp.where(mine, column, 0), 0, keepdims=True)
    return row * PAGE + lax.broadcasted_iota(jnp.int32, (1, count * PAGE), 1) % PAGE


def one_hot_rows(targets, first, rows):
    row = first + lax.broadcasted_iota(jnp.int32, (rows, targets.shape[1]), 0)
    return jnp.where(row == targets, 1.0, 0.0).astype(jnp.bfloat16)


def sublayer_kernel(
    devices, pages, reach, back,
    table_ref, frequency_ref, base_cos_ref, base_sin_ref, local_cos_ref, local_sin_ref, gain_ref,
    tokens_ref, w_kv_ref, w_query_ref, w_out_ref,
    out_ref, cache_out,
    tokens_buf, w_kv_buf, w_query_buf, w_out_buf, normed, key_own, value_own, key_in, value_in,
    tables, kv_rows, send_pages, got_pages, cosine, sine, projected, query, context,
    key_all, value_sum, low_all, right, load_sem,
    table_send, table_recv, page_send, page_recv, kv_send, kv_recv,
):
    me = lax.axis_index("seq")
    heads, rows, head_dim = query.shape
    half = head_dim // 2
    seg_rows = rows // LANES
    loads = [
        pltpu.make_async_copy(source, target, load_sem.at[i])
        for i, (source, target) in enumerate(
            [(tokens_ref, tokens_buf), (w_kv_ref, w_kv_buf), (w_query_ref, w_query_buf), (w_out_ref, w_out_buf)]
        )
    ]
    for load in loads:
        load.start()

    barrier = pltpu.get_barrier_semaphore()

    def greet(k, carry):
        pl.semaphore_signal(
            barrier, inc=1, device_id=(lax.rem(me + k, devices),), device_id_type=MESH
        )
        return carry

    lax.fori_loop(1, devices, greet, 0)

    lane = lax.broadcasted_iota(jnp.int32, (rows, head_dim), 1)
    base_cos, base_sin = base_cos_ref[pl.ds(me, 1), :], base_sin_ref[pl.ds(me, 1), :]
    local_cos, local_sin = local_cos_ref[...], local_sin_ref[...]
    cosine[...] = base_cos * local_cos - base_sin * local_sin
    stream_sin = base_sin * local_cos + base_cos * local_sin
    sine[...] = jnp.where(lane < half, -stream_sin, stream_sin)

    loads[0].wait()
    step = 128

    def norm_tile(i, carry):
        at = pl.ds(pl.multiple_of(i * step, step), step)
        wide = tokens_buf[at, :].astype(jnp.float32)
        mean_square = jnp.mean(wide * wide, -1, keepdims=True)
        normed[at, :] = (wide * lax.rsqrt(mean_square + EPS) * gain_ref[...]).astype(jnp.bfloat16)
        return carry

    lax.fori_loop(0, rows // step, norm_tile, 0)
    loads[1].wait()
    projected[...] = jnp.dot(normed[...], w_kv_buf[...], preferred_element_type=jnp.float32)

    def rotate(v):
        return v * cosine[...] + pltpu.roll(v, half, 1) * sine[...]

    key_own[...] = rotate(projected[:, :head_dim]).T.astype(jnp.bfloat16)
    value_own[...] = projected[:, head_dim:].astype(jnp.bfloat16)

    pl.semaphore_wait(barrier, devices - 1)
    kv_copies = []
    for hop in range(1, reach + 1):
        for part, (source, target) in enumerate([(key_own, key_in), (value_own, value_in)]):
            copy = pltpu.make_async_remote_copy(
                src_ref=source, dst_ref=target.at[reach - hop],
                send_sem=kv_send.at[2 * hop - 2 + part], recv_sem=kv_recv.at[2 * hop - 2 + part],
                device_id=(lax.rem(me + hop, devices),), device_id_type=MESH,
            )
            copy.start()
            kv_copies.append(copy)

    def send_table(k, carry):
        pltpu.make_async_remote_copy(
            src_ref=table_ref, dst_ref=tables.at[k - 1], send_sem=table_send, recv_sem=table_recv,
            device_id=(lax.rem(me + k, devices),), device_id_type=MESH,
        ).start()
        return carry

    lax.fori_loop(1, devices, send_table, 0)
    tables[devices - 1] = table_ref[...]

    loads[2].wait()
    pair = 2 * head_dim
    scale = head_dim ** (-0.5) * math.log2(math.e)

    def query_pair(j, carry):
        columns = pl.ds(pl.multiple_of(j * pair, pair), pair)
        part = jnp.dot(normed[...], w_query_buf[:, columns], preferred_element_type=jnp.float32)
        query[2 * j] = (rotate(part[:, :head_dim]) * scale).astype(jnp.bfloat16)
        query[2 * j + 1] = (rotate(part[:, head_dim:]) * scale).astype(jnp.bfloat16)
        return carry

    lax.fori_loop(0, heads // 2, query_pair, 0)

    table = table_ref[...]
    ids = jnp.concatenate([column_of(table[r : r + 1, :]) for r in range(seg_rows)], 0)
    below = jnp.zeros((rows, LANES), jnp.int32)
    for r in range(seg_rows):
        below = below + jnp.where(table[r : r + 1, :] < ids, 1, 0)
    local_start = jnp.sum(below, 1, keepdims=True)
    owner_column = column_of(table[seg_rows : seg_rows + 1, :])[:pages]
    order = one_hot_rows(spread(owner_column, pages), 0, devices * PAGE)

    blocks = tables.at[pl.ds(0, devices - 1)]
    pltpu.make_async_copy(blocks, blocks, table_recv).wait()
    first_id = table[0:1, 0:1]
    earlier = jnp.zeros((seg_rows, LANES), jnp.int32)
    for k in range(1, min(back, devices - 1) + 1):
        present = jnp.where(me >= k, 1, 0)
        earlier = earlier + jnp.where(tables[k - 1, 0:seg_rows, :] == first_id, present, 0)
    before = jnp.sum(jnp.sum(earlier, 1, keepdims=True), 0, keepdims=True)
    local_index = lax.broadcasted_iota(jnp.int32, (rows, 1), 0)
    start = local_start - jnp.where(ids == first_id, before, 0)
    low = jnp.maximum(start, local_index - (WINDOW - 1)) + reach * rows
    low_all[...] = jnp.broadcast_to(low, low_all.shape)

    cos_part, sin_part = cos_sin((local_index - start).astype(jnp.float32) * frequency_ref[...])
    sin_part = jnp.where(lane < half, -sin_part, sin_part)
    keys = projected[:, :head_dim]
    kv_rows[:, :head_dim] = (keys * cos_part + pltpu.roll(keys, half, 1) * sin_part).astype(jnp.bfloat16)
    kv_rows[:, head_dim:] = value_own[...]
    send_pages[...] = (
        jnp.dot(order, kv_rows[...], preferred_element_type=jnp.float32)
        .astype(jnp.bfloat16)
        .reshape(send_pages.shape)
    )

    def send_page(k, carry):
        to = lax.rem(me + k, devices)
        pltpu.make_async_remote_copy(
            src_ref=send_pages.at[to], dst_ref=got_pages.at[k - 1],
            send_sem=page_send, recv_sem=page_recv,
            device_id=(to,), device_id_type=MESH,
        ).start()
        return carry

    lax.fori_loop(1, devices, send_page, 0)
    got_pages[devices - 1] = send_pages[me]

    value_sum[reach * rows :, :head_dim] = value_own[...]
    value_sum[:, head_dim:] = jnp.ones((value_sum.shape[0], head_dim), jnp.bfloat16)
    key_all[:, reach * rows :] = key_own[...]
    for copy in kv_copies:
        copy.wait()
    for slot in range(reach):
        value_sum[slot * rows : (slot + 1) * rows, :head_dim] = value_in[slot]
        key_all[:, slot * rows : (slot + 1) * rows] = key_in[slot]
    span = WINDOW + QUERY_TILE
    extra = reach * rows
    mark = (QUERY_TILE, QUERY_TILE)
    same = lax.broadcasted_iota(jnp.int32, mark, 0) == lax.broadcasted_iota(jnp.int32, mark, 1)
    unit = jnp.where(same, 1.0, 0.0).astype(jnp.bfloat16)
    units = jnp.concatenate([unit] * HEAD_GROUP, 0)

    def tile(i, carry):
        first = pl.multiple_of(i * QUERY_TILE, QUERY_TILE)
        at = pl.ds(first, QUERY_TILE)
        shape = (QUERY_TILE, span)
        key_row = first + (extra - WINDOW) + lax.broadcasted_iota(jnp.int32, shape, 1)
        query_row = first + extra + lax.broadcasted_iota(jnp.int32, shape, 0)
        bias = jnp.where((key_row >= low_all[at, 0:1]) & (key_row <= query_row), 0.0, -1e30)
        key_at = pl.ds(pl.multiple_of(first + (extra - WINDOW), QUERY_TILE), span)
        right[:head_dim, :] = key_all[:, key_at]
        right[head_dim:, :] = bias.astype(jnp.bfloat16)

        def scores_of(g):
            left = jnp.concatenate([query[g * HEAD_GROUP + j, at, :] for j in range(HEAD_GROUP)], 0)
            return jnp.dot(
                jnp.concatenate([left, units], 1), right[...], preferred_element_type=jnp.float32
            )

        scores = scores_of(0)
        for g in range(heads // HEAD_GROUP):
            following = scores_of(g + 1) if g + 1 < heads // HEAD_GROUP else None
            peak = jnp.max(scores, 1, keepdims=True)
            weights = jnp.exp2(scores - peak).astype(jnp.bfloat16)
            both = jnp.dot(weights, value_sum[key_at, :], preferred_element_type=jnp.float32)
            mixed = (both[:, :head_dim] / both[:, head_dim:]).astype(jnp.bfloat16)
            for j in range(HEAD_GROUP):
                h = g * HEAD_GROUP + j
                context[at, h * head_dim : (h + 1) * head_dim] = mixed[
                    j * QUERY_TILE : (j + 1) * QUERY_TILE
                ]
            scores = following
        return carry

    lax.fori_loop(0, rows // QUERY_TILE, tile, 0)
    loads[3].wait()
    width = 256

    def column(j, carry):
        columns = pl.ds(pl.multiple_of(j * width, width), width)
        out_ref[:, columns] = jnp.dot(
            context[...], w_out_buf[:, columns], preferred_element_type=jnp.float32
        ).astype(jnp.bfloat16)
        return carry

    lax.fori_loop(0, out_ref.shape[1] // width, column, 0)

    owners = tables[:, seg_rows, :]
    slots = tables[:, seg_rows + 1, :]
    slot_column = jnp.sum(jnp.where(owners == me, slots + 1, 0), 1, keepdims=True) - 1
    targets = spread(slot_column, devices)
    pages_in = got_pages.at[pl.ds(0, devices - 1)]
    pltpu.make_async_copy(pages_in, pages_in, page_recv).wait()
    got = got_pages[...].reshape(devices * PAGE, 2 * head_dim)
    chunk = min(512, cache_out.shape[0])
    for c in range(cache_out.shape[0] // chunk):
        place = one_hot_rows(targets, c * chunk, chunk)
        cache_out[c * chunk : (c + 1) * chunk, :] = jnp.dot(
            place, got, preferred_element_type=jnp.float32
        ).astype(jnp.bfloat16)
    pltpu.make_async_copy(blocks, blocks, table_send).wait()
    pltpu.make_async_copy(pages_in, pages_in, page_send).wait()


def body(devices, tokens, norm_gain, w_query, w_key_value, w_out, segment_ids, page_owner, page_slot):
    rows, width = tokens.shape
    head_dim = w_key_value.shape[1] // 2
    heads = w_query.shape[1] // head_dim
    pages = rows // PAGE
    reach = WINDOW // rows
    back = MAXLEN // rows
    bf16, f32 = jnp.bfloat16, jnp.float32
    pad = jnp.full((LANES - pages,), -1, jnp.int32)
    seg_rows = rows // LANES
    table = jnp.concatenate(
        [segment_ids, page_owner, pad, page_slot, pad, jnp.zeros(((6 - seg_rows) * LANES,), jnp.int32)]
    ).reshape(8, LANES)
    half = ROPE_BASE ** (-2.0 * np.arange(head_dim // 2, dtype=np.float64) / head_dim)
    frequency = np.concatenate([half, half])[None, :]
    base = np.arange(devices, dtype=np.float64)[:, None] * rows * frequency
    local = np.arange(rows, dtype=np.float64)[:, None] * frequency
    constants = [
        jnp.asarray(c.astype(np.float32))
        for c in (frequency, np.cos(base), np.sin(base), np.cos(local), np.sin(local))
    ]
    vmem = pl.BlockSpec(memory_space=pltpu.VMEM)
    anywhere = pl.BlockSpec(memory_space=pltpu.HBM)
    dma = pltpu.SemaphoreType.DMA
    total = (reach + 1) * rows
    return pl.pallas_call(
        functools.partial(sublayer_kernel, devices, pages, reach, back),
        out_shape=(
            jax.ShapeDtypeStruct((rows, w_out.shape[1]), bf16),
            jax.ShapeDtypeStruct((devices * PAGE, 2 * head_dim), bf16),
        ),
        in_specs=[vmem] * 7 + [anywhere] * 4,
        out_specs=(vmem, vmem),
        scratch_shapes=[
            pltpu.VMEM((rows, width), bf16),
            pltpu.VMEM(w_key_value.shape, bf16),
            pltpu.VMEM(w_query.shape, bf16),
            pltpu.VMEM(w_out.shape, bf16),
            pltpu.VMEM((rows, width), bf16),
            pltpu.VMEM((head_dim, rows), bf16),
            pltpu.VMEM((rows, head_dim), bf16),
            pltpu.VMEM((reach, head_dim, rows), bf16),
            pltpu.VMEM((reach, rows, head_dim), bf16),
            pltpu.VMEM((devices, 8, LANES), jnp.int32),
            pltpu.VMEM((rows, 2 * head_dim), bf16),
            pltpu.VMEM((devices, PAGE, 2 * head_dim), bf16),
            pltpu.VMEM((devices, PAGE, 2 * head_dim), bf16),
            pltpu.VMEM((rows, head_dim), f32),
            pltpu.VMEM((rows, head_dim), f32),
            pltpu.VMEM((rows, 2 * head_dim), f32),
            pltpu.VMEM((heads, rows, head_dim), bf16),
            pltpu.VMEM((rows, heads * head_dim), bf16),
            pltpu.VMEM((head_dim, total), bf16),
            pltpu.VMEM((total, 2 * head_dim), bf16),
            pltpu.VMEM((rows, LANES), jnp.int32),
            pltpu.VMEM((head_dim + QUERY_TILE, WINDOW + QUERY_TILE), bf16),
            dma((4,)),
            dma, dma, dma, dma,
            dma((2 * reach,)), dma((2 * reach,)),
        ],
        compiler_params=pltpu.CompilerParams(
            collective_id=0, has_side_effects=True, vmem_limit_bytes=56 * 1024 * 1024
        ),
        name="attention_sublayer",
    )(table, *constants, norm_gain.reshape(1, width), tokens, w_key_value, w_query, w_out)


def solution(mesh):
    placed = (P("seq", None), P(), P(), P(), P(), P("seq"), P("seq"), P("seq"))
    return jax.shard_map(
        functools.partial(body, mesh.shape["seq"]),
        mesh=mesh,
        in_specs=placed,
        out_specs=(P("seq", None), P("seq", None)),
        check_vma=False,
    )
```

```python
import functools
import math

import jax
import jax.numpy as jnp
import numpy as np
from jax import lax
from jax.experimental import pallas as pl
from jax.experimental.pallas import tpu as pltpu
from jax.sharding import PartitionSpec as P

WINDOW = 1024
MAXLEN = 4096
PAGE = 16
EPS = 1e-06
ROPE_BASE = 10000.0
LANES = 128
QUERY_TILE = 128
HEAD_GROUP = 2
MESH = pl.DeviceIdType.MESH


def cos_sin(angles):
    turns = jnp.floor(angles * (2.0 / math.pi) + 0.5)
    c1 = 1.5703125
    c2 = float(np.float32(4.837512969970703125e-4))
    c3 = float(np.float32(7.54978995489188216e-8))
    r = ((angles - turns * c1) - turns * c2) - turns * c3
    r2 = r * r
    s = r * (1.0 + r2 * (-1.0 / 6 + r2 * (1.0 / 120 + r2 * (-1.0 / 5040))))
    c = 1.0 + r2 * (-0.5 + r2 * (1.0 / 24 + r2 * (-1.0 / 720 + r2 * (1.0 / 40320))))
    quadrant = turns.astype(jnp.int32) & 3
    odd = (quadrant & 1) == 1
    cosine = jnp.where(odd, s, c)
    sine = jnp.where(odd, c, s)
    cosine = jnp.where((quadrant == 1) | (quadrant == 2), -cosine, cosine)
    sine = jnp.where(quadrant >= 2, -sine, sine)
    return cosine, sine


def column_of(row):
    shape = (LANES, LANES)
    diagonal = lax.broadcasted_iota(jnp.int32, shape, 0) == lax.broadcasted_iota(jnp.int32, shape, 1)
    return jnp.sum(jnp.where(diagonal, jnp.broadcast_to(row, shape), 0), 1, keepdims=True)


def spread(column, count):
    shape = (count, count * PAGE)
    lane = lax.broadcasted_iota(jnp.int32, shape, 1)
    mine = (lane // PAGE) == lax.broadcasted_iota(jnp.int32, shape, 0)
    row = jnp.sum(jnp.where(mine, column, 0), 0, keepdims=True)
    return row * PAGE + lax.broadcasted_iota(jnp.int32, (1, count * PAGE), 1) % PAGE


def one_hot_rows(targets, first, rows):
    row = first + lax.broadcasted_iota(jnp.int32, (rows, targets.shape[1]), 0)
    return jnp.where(row == targets, 1.0, 0.0).astype(jnp.bfloat16)


def sublayer_kernel(
    devices, pages, reach, back,
    ids_ref, owner_ref, slot_ref, frequency_ref, gain_ref, trig_ref,
    tokens_ref, w_kv_ref, w_query_ref,
    context, pages_out, target_out,
    trig, tokens_buf, w_kv_buf, w_query_buf, normed, key_own, value_own, key_in, value_in,
    table_ref, tables, kv_rows, send_pages, got_pages, cosine, sine, projected, query,
    key_all, value_sum, low_all, right, load_sem,
    table_send, table_recv, page_send, page_recv, kv_send, kv_recv,
):
    me = lax.axis_index("seq")
    heads, rows, head_dim = query.shape
    half = head_dim // 2
    seg_rows = rows // LANES
    loads = [
        pltpu.make_async_copy(source, target, load_sem.at[i])
        for i, (source, target) in enumerate(
            [(tokens_ref, tokens_buf), (w_kv_ref, w_kv_buf), (w_query_ref, w_query_buf), (trig_ref, trig)]
        )
    ]
    for load in loads:
        load.start()

    barrier = pltpu.get_barrier_semaphore()

    def greet(k, carry):
        pl.semaphore_signal(
            barrier, inc=1, device_id=(lax.rem(me + k, devices),), device_id_type=MESH
        )
        return carry

    lax.fori_loop(1, devices, greet, 0)

    table_ref[...] = jnp.full(table_ref.shape, -1, jnp.int32)
    table_ref[0:seg_rows, :] = ids_ref[...]
    table_ref[seg_rows : seg_rows + 1, 0:pages] = owner_ref[...]
    table_ref[seg_rows + 1 : seg_rows + 2, 0:pages] = slot_ref[...]
    gain = jnp.concatenate([gain_ref[r : r + 1, :] for r in range(gain_ref.shape[0])], 1)
    loads[0].wait()
    step = 128

    def norm_tile(i, carry):
        at = pl.ds(pl.multiple_of(i * step, step), step)
        wide = tokens_buf[at, :].astype(jnp.float32)
        mean_square = jnp.mean(wide * wide, -1, keepdims=True)
        normed[at, :] = (wide * lax.rsqrt(mean_square + EPS) * gain).astype(jnp.bfloat16)
        return carry

    lax.fori_loop(0, rows // step, norm_tile, 0)
    loads[1].wait()
    projected[...] = jnp.dot(normed[...], w_kv_buf[...], preferred_element_type=jnp.float32)

    loads[3].wait()
    lane = lax.broadcasted_iota(jnp.int32, (rows, head_dim), 1)
    base_cos, base_sin = trig[pl.ds(2 * rows + me, 1), :], trig[pl.ds(2 * rows + devices + me, 1), :]
    local_cos, local_sin = trig[0:rows, :], trig[rows : 2 * rows, :]
    cosine[...] = base_cos * local_cos - base_sin * local_sin
    stream_sin = base_sin * local_cos + base_cos * local_sin
    sine[...] = jnp.where(lane < half, -stream_sin, stream_sin)

    def rotate(v):
        return v * cosine[...] + pltpu.roll(v, half, 1) * sine[...]

    key_own[...] = rotate(projected[:, :head_dim]).T.astype(jnp.bfloat16)
    value_own[...] = projected[:, head_dim:].astype(jnp.bfloat16)

    pl.semaphore_wait(barrier, devices - 1)
    def kv_hop(hop):
        return [
            pltpu.make_async_remote_copy(
                src_ref=source, dst_ref=target.at[reach - hop],
                send_sem=kv_send.at[2 * hop - 2 + part], recv_sem=kv_recv.at[2 * hop - 2 + part],
                device_id=(lax.rem(me + hop, devices),), device_id_type=MESH,
            )
            for part, (source, target) in enumerate([(key_own, key_in), (value_own, value_in)])
        ]

    for hop in range(1, reach + 1):

        @pl.when(me + hop < devices)
        def _():
            for copy in kv_hop(hop):
                copy.start()

        @pl.when(me < hop)
        def _():
            key_in[reach - hop] = jnp.zeros_like(key_own)
            value_in[reach - hop] = jnp.zeros_like(value_own)

    def send_table(k, carry):
        pltpu.make_async_remote_copy(
            src_ref=table_ref, dst_ref=tables.at[k - 1], send_sem=table_send, recv_sem=table_recv,
            device_id=(lax.rem(me + k, devices),), device_id_type=MESH,
        ).start()
        return carry

    lax.fori_loop(1, devices, send_table, 0)
    tables[devices - 1] = table_ref[...]

    loads[2].wait()
    pair = 2 * head_dim
    scale = head_dim ** (-0.5) * math.log2(math.e)

    def query_pair(j, carry):
        columns = pl.ds(pl.multiple_of(j * pair, pair), pair)
        part = jnp.dot(normed[...], w_query_buf[:, columns], preferred_element_type=jnp.float32)
        query[2 * j] = (rotate(part[:, :head_dim]) * scale).astype(jnp.bfloat16)
        query[2 * j + 1] = (rotate(part[:, head_dim:]) * scale).astype(jnp.bfloat16)
        return carry

    lax.fori_loop(0, heads // 2, query_pair, 0)

    table = table_ref[...]
    ids = jnp.concatenate([column_of(table[r : r + 1, :]) for r in range(seg_rows)], 0)
    below = jnp.zeros((rows, LANES), jnp.int32)
    for r in range(seg_rows):
        below = below + jnp.where(table[r : r + 1, :] < ids, 1, 0)
    local_start = jnp.sum(below, 1, keepdims=True)
    owner_column = column_of(table[seg_rows : seg_rows + 1, :])[:pages]
    order = one_hot_rows(spread(owner_column, pages), 0, devices * PAGE)

    blocks = tables.at[pl.ds(0, devices - 1)]
    pltpu.make_async_copy(blocks, blocks, table_recv).wait()
    first_id = table[0:1, 0:1]
    earlier = jnp.zeros((seg_rows, LANES), jnp.int32)
    for k in range(1, min(back, devices - 1) + 1):
        present = jnp.where(me >= k, 1, 0)
        earlier = earlier + jnp.where(tables[k - 1, 0:seg_rows, :] == first_id, present, 0)
    before = jnp.sum(jnp.sum(earlier, 1, keepdims=True), 0, keepdims=True)
    local_index = lax.broadcasted_iota(jnp.int32, (rows, 1), 0)
    start = local_start - jnp.where(ids == first_id, before, 0)
    low = jnp.maximum(start, local_index - (WINDOW - 1)) + reach * rows
    low_all[...] = jnp.broadcast_to(low, low_all.shape)

    cos_part, sin_part = cos_sin((local_index - start).astype(jnp.float32) * frequency_ref[...])
    sin_part = jnp.where(lane < half, -sin_part, sin_part)
    keys = projected[:, :head_dim]
    kv_rows[:, :head_dim] = (keys * cos_part + pltpu.roll(keys, half, 1) * sin_part).astype(jnp.bfloat16)
    kv_rows[:, head_dim:] = value_own[...]
    send_pages[...] = (
        jnp.dot(order, kv_rows[...], preferred_element_type=jnp.float32)
        .astype(jnp.bfloat16)
        .reshape(send_pages.shape)
    )

    def send_page(k, carry):
        to = lax.rem(me + k, devices)
        pltpu.make_async_remote_copy(
            src_ref=send_pages.at[to], dst_ref=got_pages.at[k - 1],
            send_sem=page_send, recv_sem=page_recv,
            device_id=(to,), device_id_type=MESH,
        ).start()
        return carry

    lax.fori_loop(1, devices, send_page, 0)
    got_pages[devices - 1] = send_pages[me]

    value_sum[reach * rows :, :head_dim] = value_own[...]
    value_sum[:, head_dim:] = jnp.ones((value_sum.shape[0], head_dim), jnp.bfloat16)
    key_all[:, reach * rows :] = key_own[...]
    for hop in range(1, reach + 1):

        @pl.when(me >= hop)
        def _():
            for copy in kv_hop(hop):
                copy.wait_recv()

    for slot in range(reach):
        value_sum[slot * rows : (slot + 1) * rows, :head_dim] = value_in[slot]
        key_all[:, slot * rows : (slot + 1) * rows] = key_in[slot]
    span = WINDOW + QUERY_TILE
    extra = reach * rows
    mark = (QUERY_TILE, QUERY_TILE)
    same = lax.broadcasted_iota(jnp.int32, mark, 0) == lax.broadcasted_iota(jnp.int32, mark, 1)
    unit = jnp.where(same, 1.0, 0.0).astype(jnp.bfloat16)
    units = jnp.concatenate([unit] * HEAD_GROUP, 0)

    def tile(i, carry):
        first = pl.multiple_of(i * QUERY_TILE, QUERY_TILE)
        at = pl.ds(first, QUERY_TILE)
        shape = (QUERY_TILE, span)
        key_row = first + (extra - WINDOW) + lax.broadcasted_iota(jnp.int32, shape, 1)
        query_row = first + extra + lax.broadcasted_iota(jnp.int32, shape, 0)
        bias = jnp.where((key_row >= low_all[at, 0:1]) & (key_row <= query_row), 0.0, -1e30)
        key_at = pl.ds(pl.multiple_of(first + (extra - WINDOW), QUERY_TILE), span)
        right[:head_dim, :] = key_all[:, key_at]
        right[head_dim:, :] = bias.astype(jnp.bfloat16)

        def scores_of(g):
            left = jnp.concatenate([query[g * HEAD_GROUP + j, at, :] for j in range(HEAD_GROUP)], 0)
            return jnp.dot(
                jnp.concatenate([left, units], 1), right[...], preferred_element_type=jnp.float32
            )

        scores = scores_of(0)
        for g in range(heads // HEAD_GROUP):
            following = scores_of(g + 1) if g + 1 < heads // HEAD_GROUP else None
            peak = jnp.max(scores, 1, keepdims=True)
            weights = jnp.exp2(scores - peak).astype(jnp.bfloat16)
            both = jnp.dot(weights, value_sum[key_at, :], preferred_element_type=jnp.float32)
            mixed = (both[:, :head_dim] / both[:, head_dim:]).astype(jnp.bfloat16)
            for j in range(HEAD_GROUP):
                h = g * HEAD_GROUP + j
                context[at, h * head_dim : (h + 1) * head_dim] = mixed[
                    j * QUERY_TILE : (j + 1) * QUERY_TILE
                ]
            scores = following
        return carry

    lax.fori_loop(0, rows // QUERY_TILE, tile, 0)

    owners = tables[:, seg_rows, :]
    slots = tables[:, seg_rows + 1, :]
    slot_column = jnp.sum(jnp.where(owners == me, slots + 1, 0), 1, keepdims=True) - 1
    target_out[...] = spread(slot_column, devices)
    pages_in = got_pages.at[pl.ds(0, devices - 1)]
    pltpu.make_async_copy(pages_in, pages_in, page_recv).wait()
    pages_out[...] = got_pages[...].reshape(devices * PAGE, 2 * head_dim)
    for hop in range(1, reach + 1):

        @pl.when(me + hop < devices)
        def _():
            for copy in kv_hop(hop):
                copy.wait_send()

    pltpu.make_async_copy(blocks, blocks, table_send).wait()
    pltpu.make_async_copy(pages_in, pages_in, page_send).wait()


def output_kernel(context_ref, w_out_ref, pages_ref, target_ref, out_ref, cache_out):
    out_ref[...] = jnp.dot(
        context_ref[...], w_out_ref[...], preferred_element_type=jnp.float32
    ).astype(jnp.bfloat16)

    @pl.when(pl.program_id(0) == 0)
    def _():
        chunk = min(512, cache_out.shape[0])
        for c in range(cache_out.shape[0] // chunk):
            place = one_hot_rows(target_ref[...], c * chunk, chunk)
            cache_out[c * chunk : (c + 1) * chunk, :] = jnp.dot(
                place, pages_ref[...], preferred_element_type=jnp.float32
            ).astype(jnp.bfloat16)


def body(devices, tokens, norm_gain, w_query, w_key_value, w_out, segment_ids, page_owner, page_slot):
    rows, width = tokens.shape
    head_dim = w_key_value.shape[1] // 2
    heads = w_query.shape[1] // head_dim
    pages = rows // PAGE
    reach = WINDOW // rows
    back = MAXLEN // rows
    bf16, f32 = jnp.bfloat16, jnp.float32
    half = ROPE_BASE ** (-2.0 * np.arange(head_dim // 2, dtype=np.float64) / head_dim)
    frequency = np.concatenate([half, half])[None, :]
    base = np.arange(devices, dtype=np.float64)[:, None] * rows * frequency
    local = np.arange(rows, dtype=np.float64)[:, None] * frequency
    trig = jnp.asarray(
        np.concatenate([np.cos(local), np.sin(local), np.cos(base), np.sin(base)]).astype(np.float32)
    )
    vmem = pl.BlockSpec(memory_space=pltpu.VMEM)
    anywhere = pl.BlockSpec(memory_space=pltpu.HBM)
    dma = pltpu.SemaphoreType.DMA
    total = (reach + 1) * rows
    context, got_pages, targets = pl.pallas_call(
        functools.partial(sublayer_kernel, devices, pages, reach, back),
        out_shape=(
            jax.ShapeDtypeStruct((rows, heads * head_dim), bf16),
            jax.ShapeDtypeStruct((devices * PAGE, 2 * head_dim), bf16),
            jax.ShapeDtypeStruct((1, devices * PAGE), jnp.int32),
        ),
        in_specs=[vmem] * 5 + [anywhere] * 4,
        out_specs=(vmem, vmem, vmem),
        scratch_shapes=[
            pltpu.VMEM(trig.shape, f32),
            pltpu.VMEM((rows, width), bf16),
            pltpu.VMEM(w_key_value.shape, bf16),
            pltpu.VMEM(w_query.shape, bf16),
            pltpu.VMEM((rows, width), bf16),
            pltpu.VMEM((head_dim, rows), bf16),
            pltpu.VMEM((rows, head_dim), bf16),
            pltpu.VMEM((reach, head_dim, rows), bf16),
            pltpu.VMEM((reach, rows, head_dim), bf16),
            pltpu.VMEM((8, LANES), jnp.int32),
            pltpu.VMEM((devices, 8, LANES), jnp.int32),
            pltpu.VMEM((rows, 2 * head_dim), bf16),
            pltpu.VMEM((devices, PAGE, 2 * head_dim), bf16),
            pltpu.VMEM((devices, PAGE, 2 * head_dim), bf16),
            pltpu.VMEM((rows, head_dim), f32),
            pltpu.VMEM((rows, head_dim), f32),
            pltpu.VMEM((rows, 2 * head_dim), f32),
            pltpu.VMEM((heads, rows, head_dim), bf16),
            pltpu.VMEM((head_dim, total), bf16),
            pltpu.VMEM((total, 2 * head_dim), bf16),
            pltpu.VMEM((rows, LANES), jnp.int32),
            pltpu.VMEM((head_dim + QUERY_TILE, WINDOW + QUERY_TILE), bf16),
            dma((4,)),
            dma, dma, dma, dma,
            dma((2 * reach,)), dma((2 * reach,)),
        ],
        compiler_params=pltpu.CompilerParams(
            collective_id=0, has_side_effects=True, vmem_limit_bytes=56 * 1024 * 1024
        ),
        name="attention_sublayer",
    )(
        segment_ids.reshape(rows // LANES, LANES), page_owner.reshape(1, pages), page_slot.reshape(1, pages),
        jnp.asarray(frequency.astype(np.float32)), norm_gain.reshape(width // LANES, LANES),
        trig, tokens, w_key_value, w_query,
    )
    tile = 256
    inner, wide = w_out.shape
    whole = lambda shape: pl.BlockSpec(shape, lambda j: (0, 0))
    return pl.pallas_call(
        output_kernel,
        grid=(wide // tile,),
        out_shape=(
            jax.ShapeDtypeStruct((rows, wide), bf16),
            jax.ShapeDtypeStruct(got_pages.shape, bf16),
        ),
        in_specs=[
            whole((rows, inner)),
            pl.BlockSpec((inner, tile), lambda j: (0, j)),
            whole(got_pages.shape),
            whole(targets.shape),
        ],
        out_specs=(pl.BlockSpec((rows, tile), lambda j: (0, j)), whole(got_pages.shape)),
        compiler_params=pltpu.CompilerParams(vmem_limit_bytes=24 * 1024 * 1024),
        name="output_projection",
    )(context, w_out, got_pages, targets)


def solution(mesh):
    placed = (P("seq", None), P(), P(), P(), P(), P("seq"), P("seq"), P("seq"))
    return jax.shard_map(
        functools.partial(body, mesh.shape["seq"]),
        mesh=mesh,
        in_specs=placed,
        out_specs=(P("seq", None), P("seq", None)),
        check_vma=False,
    )
```

```python
import functools
import math

import jax
import jax.numpy as jnp
import numpy as np
from jax import lax
from jax.experimental import pallas as pl
from jax.experimental.pallas import tpu as pltpu
from jax.sharding import PartitionSpec as P

WINDOW = 1024
MAXLEN = 4096
PAGE = 16
EPS = 1e-06
ROPE_BASE = 10000.0
LANES = 128
QUERY_TILE = 128
HEAD_GROUP = 4
MESH = pl.DeviceIdType.MESH


def cos_sin(angles):
    turns = jnp.floor(angles * (2.0 / math.pi) + 0.5)
    c1 = 1.5703125
    c2 = float(np.float32(4.837512969970703125e-4))
    c3 = float(np.float32(7.54978995489188216e-8))
    r = ((angles - turns * c1) - turns * c2) - turns * c3
    r2 = r * r
    s = r * (1.0 + r2 * (-1.0 / 6 + r2 * (1.0 / 120 + r2 * (-1.0 / 5040))))
    c = 1.0 + r2 * (-0.5 + r2 * (1.0 / 24 + r2 * (-1.0 / 720 + r2 * (1.0 / 40320))))
    quadrant = turns.astype(jnp.int32) & 3
    odd = (quadrant & 1) == 1
    cosine = jnp.where(odd, s, c)
    sine = jnp.where(odd, c, s)
    cosine = jnp.where((quadrant == 1) | (quadrant == 2), -cosine, cosine)
    sine = jnp.where(quadrant >= 2, -sine, sine)
    return cosine, sine


def column_of(row):
    shape = (LANES, LANES)
    diagonal = lax.broadcasted_iota(jnp.int32, shape, 0) == lax.broadcasted_iota(jnp.int32, shape, 1)
    return jnp.sum(jnp.where(diagonal, jnp.broadcast_to(row, shape), 0), 1, keepdims=True)


def spread(column, count):
    shape = (count, count * PAGE)
    lane = lax.broadcasted_iota(jnp.int32, shape, 1)
    mine = (lane // PAGE) == lax.broadcasted_iota(jnp.int32, shape, 0)
    row = jnp.sum(jnp.where(mine, column, 0), 0, keepdims=True)
    return row * PAGE + lax.broadcasted_iota(jnp.int32, (1, count * PAGE), 1) % PAGE


def one_hot_rows(targets, first, rows):
    row = first + lax.broadcasted_iota(jnp.int32, (rows, targets.shape[1]), 0)
    return jnp.where(row == targets, 1.0, 0.0).astype(jnp.bfloat16)


def sublayer_kernel(
    devices, pages, reach, back,
    ids_ref, owner_ref, slot_ref, frequency_ref, gain_ref, trig_ref,
    tokens_ref, w_kv_ref, w_query_ref,
    context, pages_out, target_out,
    trig, tokens_buf, w_kv_buf, w_query_buf, normed, key_own, value_own, key_in, value_in,
    table_ref, tables, kv_rows, send_pages, got_pages, cosine, sine, projected, query,
    key_all, value_sum, low_all, right, scores_even, scores_odd, load_sem,
    table_send, table_recv, page_send, page_recv, kv_send, kv_recv,
):
    me = lax.axis_index("seq")
    heads, rows, head_dim = query.shape
    half = head_dim // 2
    seg_rows = rows // LANES
    loads = [
        pltpu.make_async_copy(source, target, load_sem.at[i])
        for i, (source, target) in enumerate(
            [(tokens_ref, tokens_buf), (w_kv_ref, w_kv_buf), (w_query_ref, w_query_buf), (trig_ref, trig)]
        )
    ]
    for load in loads:
        load.start()

    barrier = pltpu.get_barrier_semaphore()

    def greet(k, carry):
        pl.semaphore_signal(
            barrier, inc=1, device_id=(lax.rem(me + k, devices),), device_id_type=MESH
        )
        return carry

    lax.fori_loop(1, devices, greet, 0)

    table_ref[...] = jnp.full(table_ref.shape, -1, jnp.int32)
    table_ref[0:seg_rows, :] = ids_ref[...]
    table_ref[seg_rows : seg_rows + 1, 0:pages] = owner_ref[...]
    table_ref[seg_rows + 1 : seg_rows + 2, 0:pages] = slot_ref[...]
    gain = jnp.concatenate([gain_ref[r : r + 1, :] for r in range(gain_ref.shape[0])], 1)
    loads[0].wait()
    step = 128

    def norm_tile(i, carry):
        at = pl.ds(pl.multiple_of(i * step, step), step)
        wide = tokens_buf[at, :].astype(jnp.float32)
        mean_square = jnp.mean(wide * wide, -1, keepdims=True)
        normed[at, :] = (wide * lax.rsqrt(mean_square + EPS) * gain).astype(jnp.bfloat16)
        return carry

    lax.fori_loop(0, rows // step, norm_tile, 0)
    loads[1].wait()
    projected[...] = jnp.dot(normed[...], w_kv_buf[...], preferred_element_type=jnp.float32)

    loads[3].wait()
    lane = lax.broadcasted_iota(jnp.int32, (rows, head_dim), 1)
    base_cos, base_sin = trig[pl.ds(2 * rows + me, 1), :], trig[pl.ds(2 * rows + devices + me, 1), :]
    local_cos, local_sin = trig[0:rows, :], trig[rows : 2 * rows, :]
    cosine[...] = base_cos * local_cos - base_sin * local_sin
    stream_sin = base_sin * local_cos + base_cos * local_sin
    sine[...] = jnp.where(lane < half, -stream_sin, stream_sin)

    def rotate(v):
        return v * cosine[...] + pltpu.roll(v, half, 1) * sine[...]

    key_own[...] = rotate(projected[:, :head_dim]).T.astype(jnp.bfloat16)
    value_own[...] = projected[:, head_dim:].astype(jnp.bfloat16)

    pl.semaphore_wait(barrier, devices - 1)
    def kv_hop(hop):
        return [
            pltpu.make_async_remote_copy(
                src_ref=source, dst_ref=target.at[reach - hop],
                send_sem=kv_send.at[2 * hop - 2 + part], recv_sem=kv_recv.at[2 * hop - 2 + part],
                device_id=(lax.rem(me + hop, devices),), device_id_type=MESH,
            )
            for part, (source, target) in enumerate([(key_own, key_in), (value_own, value_in)])
        ]

    for hop in range(1, reach + 1):

        @pl.when(me + hop < devices)
        def _():
            for copy in kv_hop(hop):
                copy.start()

        @pl.when(me < hop)
        def _():
            key_in[reach - hop] = jnp.zeros_like(key_own)
            value_in[reach - hop] = jnp.zeros_like(value_own)

    def send_table(k, carry):
        pltpu.make_async_remote_copy(
            src_ref=table_ref, dst_ref=tables.at[k - 1], send_sem=table_send, recv_sem=table_recv,
            device_id=(lax.rem(me + k, devices),), device_id_type=MESH,
        ).start()
        return carry

    lax.fori_loop(1, devices, send_table, 0)
    tables[devices - 1] = table_ref[...]

    loads[2].wait()
    pair = 2 * head_dim
    scale = head_dim ** (-0.5) * math.log2(math.e)

    def query_pair(j, carry):
        columns = pl.ds(pl.multiple_of(j * pair, pair), pair)
        part = jnp.dot(normed[...], w_query_buf[:, columns], preferred_element_type=jnp.float32)
        query[2 * j] = (rotate(part[:, :head_dim]) * scale).astype(jnp.bfloat16)
        query[2 * j + 1] = (rotate(part[:, head_dim:]) * scale).astype(jnp.bfloat16)
        return carry

    lax.fori_loop(0, heads // 2, query_pair, 0)

    table = table_ref[...]
    ids = jnp.concatenate([column_of(table[r : r + 1, :]) for r in range(seg_rows)], 0)
    below = jnp.zeros((rows, LANES), jnp.int32)
    for r in range(seg_rows):
        below = below + jnp.where(table[r : r + 1, :] < ids, 1, 0)
    local_start = jnp.sum(below, 1, keepdims=True)
    owner_column = column_of(table[seg_rows : seg_rows + 1, :])[:pages]
    order = one_hot_rows(spread(owner_column, pages), 0, devices * PAGE)

    blocks = tables.at[pl.ds(0, devices - 1)]
    pltpu.make_async_copy(blocks, blocks, table_recv).wait()
    first_id = table[0:1, 0:1]
    earlier = jnp.zeros((seg_rows, LANES), jnp.int32)
    for k in range(1, min(back, devices - 1) + 1):
        present = jnp.where(me >= k, 1, 0)
        earlier = earlier + jnp.where(tables[k - 1, 0:seg_rows, :] == first_id, present, 0)
    before = jnp.sum(jnp.sum(earlier, 1, keepdims=True), 0, keepdims=True)
    local_index = lax.broadcasted_iota(jnp.int32, (rows, 1), 0)
    start = local_start - jnp.where(ids == first_id, before, 0)
    low = jnp.maximum(start, local_index - (WINDOW - 1)) + reach * rows
    low_all[...] = jnp.broadcast_to(low, low_all.shape)

    cos_part, sin_part = cos_sin((local_index - start).astype(jnp.float32) * frequency_ref[...])
    sin_part = jnp.where(lane < half, -sin_part, sin_part)
    keys = projected[:, :head_dim]
    kv_rows[:, :head_dim] = (keys * cos_part + pltpu.roll(keys, half, 1) * sin_part).astype(jnp.bfloat16)
    kv_rows[:, head_dim:] = value_own[...]
    send_pages[...] = (
        jnp.dot(order, kv_rows[...], preferred_element_type=jnp.float32)
        .astype(jnp.bfloat16)
        .reshape(send_pages.shape)
    )

    def send_page(k, carry):
        to = lax.rem(me + k, devices)
        pltpu.make_async_remote_copy(
            src_ref=send_pages.at[to], dst_ref=got_pages.at[k - 1],
            send_sem=page_send, recv_sem=page_recv,
            device_id=(to,), device_id_type=MESH,
        ).start()
        return carry

    lax.fori_loop(1, devices, send_page, 0)
    got_pages[devices - 1] = send_pages[me]

    span = WINDOW + QUERY_TILE
    extra = reach * rows
    tiles = rows // QUERY_TILE

    def mask_tile(i, carry):
        first = pl.multiple_of(i * QUERY_TILE, QUERY_TILE)
        shape = (QUERY_TILE, span)
        key_row = first + (extra - WINDOW) + lax.broadcasted_iota(jnp.int32, shape, 1)
        query_row = first + extra + lax.broadcasted_iota(jnp.int32, shape, 0)
        seen = (key_row >= low_all[pl.ds(first, QUERY_TILE), 0:1]) & (key_row <= query_row)
        right[i, head_dim:, :] = jnp.where(seen, 0.0, -1e30).astype(jnp.bfloat16)
        return carry

    lax.fori_loop(0, tiles, mask_tile, 0)
    value_sum[extra:, :head_dim] = value_own[...]
    value_sum[:, head_dim:] = jnp.ones((value_sum.shape[0], head_dim), jnp.bfloat16)
    key_all[:, extra:] = key_own[...]
    mark = (QUERY_TILE, QUERY_TILE)
    same = lax.broadcasted_iota(jnp.int32, mark, 0) == lax.broadcasted_iota(jnp.int32, mark, 1)
    unit = jnp.where(same, 1.0, 0.0).astype(jnp.bfloat16)
    units = jnp.concatenate([unit] * HEAD_GROUP, 0)
    for hop in range(1, reach + 1):

        @pl.when(me >= hop)
        def _():
            for copy in kv_hop(hop):
                copy.wait_recv()

    for slot in range(reach):
        value_sum[slot * rows : (slot + 1) * rows, :head_dim] = value_in[slot]
        key_all[:, slot * rows : (slot + 1) * rows] = key_in[slot]
    for i in range(tiles):
        first = i * QUERY_TILE + extra - WINDOW
        right[i, :head_dim, :] = key_all[:, first : first + span]

    groups = heads // HEAD_GROUP
    stages = tiles * groups

    def put_scores(n, target):
        i, g = lax.div(n, groups), lax.rem(n, groups)
        at = pl.ds(pl.multiple_of(i * QUERY_TILE, QUERY_TILE), QUERY_TILE)
        left = jnp.concatenate([query[g * HEAD_GROUP + j, at, :] for j in range(HEAD_GROUP)], 0)
        target[...] = jnp.dot(
            jnp.concatenate([left, units], 1), right[i], preferred_element_type=jnp.float32
        )

    def attend(n, source):
        i, g = lax.div(n, groups), lax.rem(n, groups)
        first = pl.multiple_of(i * QUERY_TILE, QUERY_TILE)
        scores = source[...]
        peak = jnp.max(scores, 1, keepdims=True)
        weights = jnp.exp2(scores - peak).astype(jnp.bfloat16)
        values = value_sum[pl.ds(pl.multiple_of(first + (extra - WINDOW), QUERY_TILE), span), :]
        both = jnp.dot(weights, values, preferred_element_type=jnp.float32)
        mixed = (both[:, :head_dim] / both[:, head_dim:]).astype(jnp.bfloat16)
        for j in range(HEAD_GROUP):
            column = pl.multiple_of((g * HEAD_GROUP + j) * head_dim, head_dim)
            context[pl.ds(first, QUERY_TILE), pl.ds(column, head_dim)] = mixed[
                j * QUERY_TILE : (j + 1) * QUERY_TILE
            ]

    put_scores(jnp.int32(0), scores_even)

    def two_stages(k, carry):
        put_scores(2 * k + 1, scores_odd)
        attend(2 * k, scores_even)
        put_scores(2 * k + 2, scores_even)
        attend(2 * k + 1, scores_odd)
        return carry

    lax.fori_loop(0, stages // 2 - 1, two_stages, 0)
    put_scores(jnp.int32(stages - 1), scores_odd)
    attend(jnp.int32(stages - 2), scores_even)
    attend(jnp.int32(stages - 1), scores_odd)

    owners = tables[:, seg_rows, :]
    slots = tables[:, seg_rows + 1, :]
    slot_column = jnp.sum(jnp.where(owners == me, slots + 1, 0), 1, keepdims=True) - 1
    target_out[...] = spread(slot_column, devices)
    pages_in = got_pages.at[pl.ds(0, devices - 1)]
    pltpu.make_async_copy(pages_in, pages_in, page_recv).wait()
    pages_out[...] = got_pages[...].reshape(devices * PAGE, 2 * head_dim)
    for hop in range(1, reach + 1):

        @pl.when(me + hop < devices)
        def _():
            for copy in kv_hop(hop):
                copy.wait_send()

    pltpu.make_async_copy(blocks, blocks, table_send).wait()
    pltpu.make_async_copy(pages_in, pages_in, page_send).wait()


def output_kernel(context_ref, w_out_ref, pages_ref, target_ref, out_ref, cache_out):
    out_ref[...] = jnp.dot(
        context_ref[...], w_out_ref[...], preferred_element_type=jnp.float32
    ).astype(jnp.bfloat16)

    @pl.when(pl.program_id(0) == 0)
    def _():
        chunk = min(512, cache_out.shape[0])
        for c in range(cache_out.shape[0] // chunk):
            place = one_hot_rows(target_ref[...], c * chunk, chunk)
            cache_out[c * chunk : (c + 1) * chunk, :] = jnp.dot(
                place, pages_ref[...], preferred_element_type=jnp.float32
            ).astype(jnp.bfloat16)


def body(devices, tokens, norm_gain, w_query, w_key_value, w_out, segment_ids, page_owner, page_slot):
    rows, width = tokens.shape
    head_dim = w_key_value.shape[1] // 2
    heads = w_query.shape[1] // head_dim
    pages = rows // PAGE
    reach = WINDOW // rows
    back = MAXLEN // rows
    bf16, f32 = jnp.bfloat16, jnp.float32
    half = ROPE_BASE ** (-2.0 * np.arange(head_dim // 2, dtype=np.float64) / head_dim)
    frequency = np.concatenate([half, half])[None, :]
    base = np.arange(devices, dtype=np.float64)[:, None] * rows * frequency
    local = np.arange(rows, dtype=np.float64)[:, None] * frequency
    trig = jnp.asarray(
        np.concatenate([np.cos(local), np.sin(local), np.cos(base), np.sin(base)]).astype(np.float32)
    )
    vmem = pl.BlockSpec(memory_space=pltpu.VMEM)
    anywhere = pl.BlockSpec(memory_space=pltpu.HBM)
    dma = pltpu.SemaphoreType.DMA
    total = (reach + 1) * rows
    context, got_pages, targets = pl.pallas_call(
        functools.partial(sublayer_kernel, devices, pages, reach, back),
        out_shape=(
            jax.ShapeDtypeStruct((rows, heads * head_dim), bf16),
            jax.ShapeDtypeStruct((devices * PAGE, 2 * head_dim), bf16),
            jax.ShapeDtypeStruct((1, devices * PAGE), jnp.int32),
        ),
        in_specs=[vmem] * 5 + [anywhere] * 4,
        out_specs=(vmem, vmem, vmem),
        scratch_shapes=[
            pltpu.VMEM(trig.shape, f32),
            pltpu.VMEM((rows, width), bf16),
            pltpu.VMEM(w_key_value.shape, bf16),
            pltpu.VMEM(w_query.shape, bf16),
            pltpu.VMEM((rows, width), bf16),
            pltpu.VMEM((head_dim, rows), bf16),
            pltpu.VMEM((rows, head_dim), bf16),
            pltpu.VMEM((reach, head_dim, rows), bf16),
            pltpu.VMEM((reach, rows, head_dim), bf16),
            pltpu.VMEM((8, LANES), jnp.int32),
            pltpu.VMEM((devices, 8, LANES), jnp.int32),
            pltpu.VMEM((rows, 2 * head_dim), bf16),
            pltpu.VMEM((devices, PAGE, 2 * head_dim), bf16),
            pltpu.VMEM((devices, PAGE, 2 * head_dim), bf16),
            pltpu.VMEM((rows, head_dim), f32),
            pltpu.VMEM((rows, head_dim), f32),
            pltpu.VMEM((rows, 2 * head_dim), f32),
            pltpu.VMEM((heads, rows, head_dim), bf16),
            pltpu.VMEM((head_dim, total), bf16),
            pltpu.VMEM((total, 2 * head_dim), bf16),
            pltpu.VMEM((rows, LANES), jnp.int32),
            pltpu.VMEM((rows // QUERY_TILE, head_dim + QUERY_TILE, WINDOW + QUERY_TILE), bf16),
            pltpu.VMEM((HEAD_GROUP * QUERY_TILE, WINDOW + QUERY_TILE), f32),
            pltpu.VMEM((HEAD_GROUP * QUERY_TILE, WINDOW + QUERY_TILE), f32),
            dma((4,)),
            dma, dma, dma, dma,
            dma((2 * reach,)), dma((2 * reach,)),
        ],
        compiler_params=pltpu.CompilerParams(
            collective_id=0, has_side_effects=True, vmem_limit_bytes=56 * 1024 * 1024
        ),
        name="attention_sublayer",
    )(
        segment_ids.reshape(rows // LANES, LANES), page_owner.reshape(1, pages), page_slot.reshape(1, pages),
        jnp.asarray(frequency.astype(np.float32)), norm_gain.reshape(width // LANES, LANES),
        trig, tokens, w_key_value, w_query,
    )
    tile = 512
    inner, wide = w_out.shape
    whole = lambda shape: pl.BlockSpec(shape, lambda j: (0, 0))
    return pl.pallas_call(
        output_kernel,
        grid=(wide // tile,),
        out_shape=(
            jax.ShapeDtypeStruct((rows, wide), bf16),
            jax.ShapeDtypeStruct(got_pages.shape, bf16),
        ),
        in_specs=[
            whole((rows, inner)),
            pl.BlockSpec((inner, tile), lambda j: (0, j)),
            whole(got_pages.shape),
            whole(targets.shape),
        ],
        out_specs=(pl.BlockSpec((rows, tile), lambda j: (0, j)), whole(got_pages.shape)),
        compiler_params=pltpu.CompilerParams(vmem_limit_bytes=60 * 1024 * 1024),
        name="output_projection",
    )(context, w_out, got_pages, targets)


def solution(mesh):
    placed = (P("seq", None), P(), P(), P(), P(), P("seq"), P("seq"), P("seq"))
    return jax.shard_map(
        functools.partial(body, mesh.shape["seq"]),
        mesh=mesh,
        in_specs=placed,
        out_specs=(P("seq", None), P("seq", None)),
        check_vma=False,
    )
```
